32 devices in a mesh: dp: 16 (over z, x, core), tensor: 2 (over y).
Axes of the slice: x: 2, y: 2, z: 4, core: 2. Of those that a mesh axis runs over, the one named last changes fastest.
Arguments:
- tokens: bfloat16 [16384, 1024], P(('dp', 'tensor')), may hold values from -6 to 6
- gain_attn: bfloat16 [1024], P(('dp', 'tensor')), may hold values from 0.5 to 1.5
- gain_ffn: bfloat16 [1024], P(('dp', 'tensor')), may hold values from 0.5 to 1.5
- w_query: bfloat16 [1024, 1024], P('dp', 'tensor'), may hold values from -0.75 to 0.75
- w_key: bfloat16 [1024, 512], P('dp', 'tensor'), may hold values from -0.75 to 0.75
- w_value: bfloat16 [1024, 512], P('dp', 'tensor'), may hold values from -0.1875 to 0.1875
- w_output: bfloat16 [1024, 1024], P('tensor', 'dp'), may hold values from -2 to 2
- w_router: bfloat16 [1024, 16], P(('dp', 'tensor')), may hold values from -0.09375 to 0.09375
- w_gate: bfloat16 [16, 1024, 512], P(None, 'dp', 'tensor'), may hold values from -0.1875 to 0.1875
- w_up: bfloat16 [16, 1024, 512], P(None, 'dp', 'tensor'), may hold values from -0.1875 to 0.1875
- w_down: bfloat16 [16, 512, 1024], P(None, 'tensor', 'dp'), may hold values from -4 to 4
- segments: int32 [16384], P('dp'), may hold values from 0 to 2, as said below
- routes: int32 [16384, 8], P('dp'), may hold values from 0 to 15, all different within a row; in each aligned block of 1024 rows (0 to 1023, 1024 to 2047, ...) at most 640 rows name the same one
- cotangent: bfloat16 [16384, 1024], P(('dp', 'tensor')), may hold values from -6 to 6
Outputs:
- output: float32 [16384, 1024], P(('dp', 'tensor'))
- grad_tokens: float32 [16384, 1024], P(('dp', 'tensor'))
- grad_gain_attn: float32 [1024], P(('dp', 'tensor'))
- grad_gain_ffn: float32 [1024], P(('dp', 'tensor'))
- grad_query: float32 [1024, 1024], P('dp', 'tensor')
- grad_key: float32 [1024, 512], P('dp', 'tensor')
- grad_value: float32 [1024, 512], P('dp', 'tensor')
- grad_output: float32 [1024, 1024], P('tensor', 'dp')
- grad_router: float32 [1024, 16], P(('dp', 'tensor'))
- grad_gate: float32 [16, 1024, 512], P(None, 'dp', 'tensor')
- grad_up: float32 [16, 1024, 512], P(None, 'dp', 'tensor')
- grad_down: float32 [16, 512, 1024], P(None, 'tensor', 'dp')
The draws below stay inside these ranges and needn't reach their ends.
Inputs may be any that keep to these rules, and one draw needn't show every extreme that they name: `segments`: document numbers restart at 0 in each block of 1024 tokens of one index of dp and never fall within it; each block holds 3 documents. `routes`: within the 1024 tokens of one index of dp, no expert is named by more than 640 tokens.
All inputs are finite; a program needn't handle non-finite values.
Results may differ from the reference program's by a relative error of at most 0.02.
Values may be sent and summed in bfloat16 or wider, within the bound.
A program may use at most 384 MiB of HBM per device.

```python
import math
import jax
import jax.numpy as jnp
import numpy as np
from jax import lax

D = 1024
HEADS = 16
KV_HEADS = 8
HEAD = 64
FF = 512
TOP = 8
EXPERTS = 16
SEGS = 3
TOK_DEV = 1024
TOKENS = 16384
CAP = 640


def draw_segments(key, part):
    key = jax.random.fold_in(key, 11)
    groups = TOKENS // TOK_DEV
    low_edge = TOK_DEV // 2 - TOK_DEV // 8
    high_edge = TOK_DEV // 2 + TOK_DEV // 8
    candidates = jnp.concatenate([jnp.arange(1, low_edge, dtype=jnp.int32), jnp.arange(high_edge + 1, TOK_DEV, dtype=jnp.int32)])
    index_row = jnp.arange(TOK_DEV, dtype=jnp.int32)

    def one_group(group_key):
        shuffled = jax.random.permutation(group_key, candidates.shape[0])
        cut_points = candidates[shuffled[:SEGS - 1]]
        return jnp.sum((index_row[:, None] >= cut_points[None, :]).astype(jnp.int32), axis=1).astype(jnp.int32)
    group_keys = jax.random.split(key, groups)
    return jax.vmap(one_group)(group_keys).reshape(TOKENS)


def block_scale(rng, dims, cuts, smallest, largest):
    loudness, own = 1.0, jax.random.fold_in(rng, 6)
    for dim, blocks in cuts:
        heights = jnp.exp(jax.random.uniform(jax.random.fold_in(own, dim), (blocks,), jnp.float32, smallest / len(cuts), largest / len(cuts)))
        loudness = loudness * jnp.repeat(heights, dims[dim] // blocks).reshape([-1 if axis == dim else 1 for axis in range(len(dims))])
    return loudness


def assign_block(key, own, number, rows, count, top, most, slope):
    order = jax.random.permutation(key, count)
    packed, ordinary = shares(count, rows * top, most, slope, True), shares(count, rows * top, most, slope, False)
    places = jnp.arange(count)

    def named(lengths, offset_by):
        used = int((lengths > 0).sum())
        fixed = max(1, used // 4)
        shifted = fixed + (places - fixed + offset_by * (used - fixed)) % max(1, count - fixed)
        return jnp.zeros((count,), jnp.int32).at[order[jnp.where(places < fixed, places, shifted)]].set(jnp.asarray(lengths, jnp.int32))

    lengths = jnp.where(number % 4 == 0, named(packed, number // 4), named(ordinary, number - number // 4 - 1))
    mixed = jax.random.permutation(jax.random.fold_in(own, 3), count)
    donor, receiver = mixed[0:count // 2 * 2:2], mixed[1:count // 2 * 2:2]
    slack = jnp.minimum(lengths[donor] - 1, most - lengths[receiver]) // 2
    slack = jnp.where((donor == order[0]) | (receiver == order[0]) | (lengths[receiver] == 0), 0, jnp.maximum(slack, 0))
    shifted = jax.random.randint(jax.random.fold_in(own, 4), (count // 2,), 0, 1 << 20) % (slack + 1)
    lengths = lengths.at[donor].add(-shifted).at[receiver].add(shifted)
    items = jnp.searchsorted(jnp.cumsum(lengths), jnp.arange(rows * top), side="right").astype(jnp.int32)
    listing = items.reshape(top, rows).T
    listing = listing[jax.random.permutation(jax.random.fold_in(own, 1), rows)]
    offset_by = jax.random.randint(jax.random.fold_in(own, 2), (rows, 1), 0, top)
    return jnp.take_along_axis(listing, (jnp.arange(top)[None, :] + offset_by) % top, axis=1)


def shares(count, total, most, slope, full):
    portions = [(1 << 20) // math.isqrt(rank ** slope) + 1 for rank in range(1, count + 1)]
    largest = most if full else min(most, max(-(-total // count), total * portions[0] // sum(portions)))
    least = 1 if total - largest >= count - 1 else 0
    holding, rest = [largest] + [least] * (count - 1), total - largest - least * (count - 1)
    while rest > 0:
        movable = [i for i in range(1, count) if holding[i] < largest] or [i for i in range(1, count) if holding[i] < most]
        mass, left = sum([portions[i] for i in movable]), rest
        for i in movable:
            addition = min(most - holding[i], max(1, left * portions[i] // mass), rest)
            holding[i] = holding[i] + addition
            rest = rest - addition
    return np.array(holding)


def bell_draw(own_key, dims, spread, reach, cuts=(), kind=jnp.bfloat16):
    values = jax.random.normal(own_key, dims, jnp.float32) * spread
    if len(cuts) > 0:
        values = block_scale(own_key, dims, cuts, -0.22, 0.18) * values
    return jnp.clip(values, min=-reach, max=reach).astype(kind)


def setup_inputs(seed: int = 0) -> dict:
    streams_of = jax.random.split(jax.random.key(seed), 15)
    tokens = bell_draw(streams_of[0], (TOKENS, D), 1.0, 6.0, ((0, 32),))
    gain_attn = jnp.clip(1.0 + 0.1 * jax.random.normal(streams_of[1], (D,), jnp.float32), 0.5, 1.5).astype(jnp.bfloat16)
    gain_ffn = jnp.clip(1.0 + 0.1 * jax.random.normal(streams_of[2], (D,), jnp.float32), 0.5, 1.5).astype(jnp.bfloat16)
    w_query = bell_draw(streams_of[3], (D, HEADS * HEAD), (D // 16) ** -0.5, 0.75, ((0, 16), (1, 2)))
    w_key = bell_draw(streams_of[4], (D, KV_HEADS * HEAD), (D // 16) ** -0.5, 0.75, ((0, 16), (1, 2)))
    w_value = bell_draw(streams_of[5], (D, KV_HEADS * HEAD), D ** -0.5, 0.1875, ((0, 16), (1, 2)))
    w_output = bell_draw(streams_of[6], (HEADS * HEAD, D), (max(HEADS * HEAD // 128, 1)) ** -0.5, 2.0, ((0, 2), (1, 16)))
    w_router = bell_draw(streams_of[7], (D, EXPERTS), (4 * D) ** -0.5, 0.09375, ((0, 32),))
    w_gate = bell_draw(streams_of[8], (EXPERTS, D, FF), D ** -0.5, 0.1875, ((1, 16), (2, 2)))
    w_up = bell_draw(streams_of[9], (EXPERTS, D, FF), D ** -0.5, 0.1875, ((1, 16), (2, 2)))
    w_down = bell_draw(streams_of[10], (EXPERTS, FF, D), (max(FF // 256, 1)) ** -0.5, 4.0, ((1, 2), (2, 16)))
    segments = draw_segments(jax.random.fold_in(streams_of[14], 71), 0)
    routes_keys = jax.random.split(jax.random.fold_in(streams_of[12], 1), TOKENS // TOK_DEV)
    routes_turns = jax.random.permutation(jax.random.fold_in(streams_of[12], 3), TOKENS // TOK_DEV)
    routes = jax.vmap(lambda own, number: assign_block(jax.random.fold_in(streams_of[12], 2), own, number, TOK_DEV, EXPERTS, TOP, CAP, 1))(routes_keys, routes_turns).reshape((TOKENS, TOP))
    cotangent = bell_draw(streams_of[13], (TOKENS, D), 1.0, 6.0, ((0, 32),))
    return {"tokens": tokens, "gain_attn": gain_attn, "gain_ffn": gain_ffn, "w_query": w_query, "w_key": w_key, "w_value": w_value, "w_output": w_output, "w_router": w_router, "w_gate": w_gate, "w_up": w_up, "w_down": w_down, "segments": segments, "routes": routes, "cotangent": cotangent}


EPSILON = 1e-06
RESIDUAL_SCALE = 0.22
SCORE_SCALE = 0.015625
MASKED = -1e+30
PRECISE = lax.Precision.HIGHEST

@jax.custom_vjp
def low(v):
    return lax.optimization_barrier(v.astype(jnp.bfloat16)).astype(jnp.float32)

@jax.custom_vjp
def low_back(v):
    return v

def low_keep(v):
    return (low(v), None)

def low_pass(kept, grad):
    return (grad,)

def back_keep(v):
    return (v, None)

def back_low(kept, grad):
    return (low(grad),)
low.defvjp(low_keep, low_pass)
low_back.defvjp(back_keep, back_low)

def positions(doc_ids):
    index_row = jnp.arange(doc_ids.shape[0], dtype=jnp.int32)
    starting = jnp.concatenate([jnp.ones((1,), dtype=jnp.bool_), doc_ids[1:] != doc_ids[:-1]])
    seg_begin = lax.cummax(jnp.where(starting, index_row, jnp.zeros_like(index_row)), axis=0)
    return index_row - seg_begin

def rotary(places, half_width):
    freqs = 10000.0 ** (-jnp.arange(half_width, dtype=jnp.float32) / half_width)
    angles = places.astype(jnp.float32)[:, None] * freqs[None, :]
    return (jnp.cos(angles)[:, None, :], jnp.sin(angles)[:, None, :])

def rotate(values, cosine, sine):
    half_width = values.shape[-1] // 2
    first_half = values[..., :half_width]
    second_half = values[..., half_width:]
    return jnp.concatenate([first_half * cosine - second_half * sine, second_half * cosine + first_half * sine], axis=-1)

def rms_norm(values, gain):
    return values * lax.rsqrt(lax.optimization_barrier(jnp.mean(values * values, axis=-1, keepdims=True)) + EPSILON) * gain

def layer_block(inputs, doc_ids, picks, weights):
    gain_one, gain_two, query_w, key_w, value_w, out_w, router_w, gate_w, up_w, down_w = weights
    count_rows = inputs.shape[0]
    repeat = HEADS // KV_HEADS
    cosine, sine = rotary(positions(doc_ids), HEAD // 2)
    normed_one = low(rms_norm(inputs, gain_one))
    query_lin = low_back(jnp.dot(normed_one, query_w, precision=PRECISE)).reshape(count_rows, HEADS, HEAD)
    key_lin = low_back(jnp.dot(normed_one, key_w, precision=PRECISE)).reshape(count_rows, KV_HEADS, HEAD)
    values = low(low_back(jnp.dot(normed_one, value_w, precision=PRECISE))).reshape(count_rows, KV_HEADS, HEAD)
    queries = low(rotate(query_lin, cosine, sine)).reshape(count_rows, KV_HEADS, repeat, HEAD)
    keys = low(rotate(key_lin, cosine, sine))
    scores = low_back(jnp.einsum('igrd,jgd->grij', queries, keys, precision=PRECISE)) * SCORE_SCALE
    index_row = jnp.arange(count_rows, dtype=jnp.int32)
    allowed = (doc_ids[:, None] == doc_ids[None, :]) & (index_row[None, :] <= index_row[:, None])
    scores = jnp.where(allowed, scores, MASKED)
    probs = jax.nn.softmax(scores, axis=-1)
    mixed = jnp.einsum('grij,jgd->igrd', low(probs), values, precision=PRECISE).reshape(count_rows, HEADS * HEAD)
    mixed = low(low_back(mixed))
    after_attn = inputs + RESIDUAL_SCALE * low_back(jnp.dot(mixed, out_w, precision=PRECISE))
    normed_two = low(rms_norm(after_attn, gain_two))
    logits = jnp.dot(normed_two, router_w, precision=PRECISE)
    onehot = (picks[:, :, None] == jnp.arange(EXPERTS, dtype=jnp.int32)[None, None, :]).astype(jnp.float32)
    chosen = jnp.einsum('tke,te->tk', onehot, logits, precision=PRECISE)
    gates = jax.nn.softmax(chosen, axis=-1)
    combine = jnp.einsum('tk,tke->te', gates, onehot, precision=PRECISE)
    gate_pre = low_back(jnp.einsum('td,edf->etf', normed_two, gate_w, precision=PRECISE))
    up_pre = low_back(jnp.einsum('td,edf->etf', normed_two, up_w, precision=PRECISE))
    hidden = low(jax.nn.silu(gate_pre) * up_pre)
    expert_out = low_back(jnp.einsum('etf,efd->etd', hidden, down_w, precision=PRECISE))
    moe_out = jnp.einsum('te,etd->td', combine, expert_out, precision=PRECISE)
    return after_attn + RESIDUAL_SCALE * low_back(moe_out)

def reference(tokens, gain_attn, gain_ffn, w_query, w_key, w_value, w_output, w_router, w_gate, w_up, w_down, segments, routes, cotangent):
    inputs = tokens.astype(jnp.float32)
    params = tuple((item.astype(jnp.float32) for item in (gain_attn, gain_ffn, w_query, w_key, w_value, w_output, w_router, w_gate, w_up, w_down)))
    groups = inputs.shape[0] // TOK_DEV
    doc_blocks = segments.reshape(groups, TOK_DEV)
    pick_blocks = routes.reshape(groups, TOK_DEV, TOP)
    saved_block = jax.checkpoint(layer_block)

    def forward(inputs, *weights):

        def step_fn(carry, item):
            return (carry, saved_block(item[0], item[1], item[2], weights))
        carry, result = lax.scan(step_fn, jnp.zeros((), jnp.float32), (inputs.reshape(groups, TOK_DEV, D), doc_blocks, pick_blocks))
        return result.reshape(groups * TOK_DEV, D)
    output, pullback = jax.vjp(forward, inputs, *params)
    grads = pullback(cotangent.astype(jnp.float32))
    return (output, grads[0], grads[1], grads[2], grads[3], grads[4], grads[5], grads[6], grads[7], grads[8], grads[9], grads[10])
```

```python
import jax
import jax.numpy as jnp
from jax import lax
from jax.experimental import pallas as pl
from jax.experimental.pallas import tpu as pltpu
from jax.sharding import PartitionSpec as P

HEAD = 64
BLOCK = 256


EPSILON = 1e-06
RESIDUAL_SCALE = 0.22
SCORE_SCALE = 0.015625
MASKED = -1e30


def positions(doc_ids):
    index_row = jnp.arange(doc_ids.shape[0], dtype=jnp.int32)
    starting = jnp.concatenate([jnp.ones((1,), dtype=jnp.bool_), doc_ids[1:] != doc_ids[:-1]])
    seg_begin = lax.cummax(jnp.where(starting, index_row, jnp.zeros_like(index_row)), axis=0)
    return index_row - seg_begin


def rotary(places, half_width):
    freqs = 10000.0 ** (-jnp.arange(half_width, dtype=jnp.float32) / half_width)
    angles = freqs[:, None] * places.astype(jnp.float32)[None, :]
    return (jnp.cos(angles), jnp.sin(angles))


def rotate(values, cosine, sine):
    heads = values.reshape(values.shape[0] // HEAD, 2, HEAD // 2, values.shape[1])
    first_half, second_half = heads[:, 0], heads[:, 1]
    return jnp.stack(
        [first_half * cosine - second_half * sine, second_half * cosine + first_half * sine],
        axis=1,
    ).reshape(values.shape)


def norm_back(grad_normed, base, inverse, gain):
    scaled = grad_normed * gain
    return inverse * scaled - base * inverse * jnp.mean(scaled * base, axis=-1, keepdims=True)


def dot(left, right, left_dim=1, right_dim=0):
    return lax.dot_general(
        left, right, (((left_dim,), (right_dim,)), ((), ())), preferred_element_type=jnp.float32
    )


def transposed_dot(left, right):
    return dot(left, right, 1, 1)


def allowed_keys(begin_ref, start, stop):
    shape = (stop, stop - start)
    key = lax.broadcasted_iota(jnp.int32, shape, 0)
    query = lax.broadcasted_iota(jnp.int32, shape, 1) + start
    return (key >= begin_ref[:, start:stop]) & (key <= query)


def attend_kernel(begin_ref, query_ref, key_ref, value_ref, mixed_ref, lse_ref):
    total = key_ref.shape[1]
    keys = (key_ref[...].astype(jnp.float32) * SCORE_SCALE).T.astype(jnp.bfloat16)
    for start in range(0, total, BLOCK):
        stop = start + BLOCK
        allowed = allowed_keys(begin_ref, start, stop)
        for head in range(query_ref.shape[0] // HEAD):
            rows = slice(head * HEAD, (head + 1) * HEAD)
            scores = dot(keys[:stop], query_ref[rows, start:stop])
            scores = jnp.where(allowed, scores, MASKED)
            top = jnp.max(scores, axis=0, keepdims=True)
            expo = jnp.exp(scores - top)
            denom = jnp.sum(expo, axis=0, keepdims=True)
            probs = (expo * (1.0 / denom)).astype(jnp.bfloat16)
            mixed_ref[rows, start:stop] = dot(value_ref[:, :stop], probs).astype(jnp.bfloat16)
            lse_ref[0, head : head + 1, start:stop] = top + jnp.log(denom)


def attend_back_kernel(
    begin_ref,
    query_ref,
    key_ref,
    value_ref,
    lse_ref,
    grad_ref,
    grad_query_ref,
    grad_key_ref,
    grad_value_ref,
):
    total = key_ref.shape[1]
    keys = (key_ref[...].astype(jnp.float32) * SCORE_SCALE).T.astype(jnp.bfloat16)
    values = value_ref[...].astype(jnp.float32).T.astype(jnp.bfloat16)
    grad_key_ref[...] = jnp.zeros_like(grad_key_ref)
    grad_value_ref[...] = jnp.zeros_like(grad_value_ref)
    for start in range(0, total, BLOCK):
        stop = start + BLOCK
        allowed = allowed_keys(begin_ref, start, stop)
        for head in range(query_ref.shape[0] // HEAD):
            rows = slice(head * HEAD, (head + 1) * HEAD)
            query = query_ref[rows, start:stop]
            grad = grad_ref[rows, start:stop]
            scores = dot(keys[:stop], query) - lse_ref[0, head : head + 1, start:stop]
            probs = jnp.exp(jnp.where(allowed, scores, MASKED))
            grad_probs = dot(values[:stop], grad)
            delta = jnp.sum(probs * grad_probs, axis=0, keepdims=True)
            grad_scores = (probs * (grad_probs - delta)).astype(jnp.bfloat16)
            grad_query_ref[rows, start:stop] = SCORE_SCALE * dot(key_ref[:, :stop], grad_scores)
            grad_key_ref[:, :stop] += SCORE_SCALE * transposed_dot(query, grad_scores)
            grad_value_ref[:, :stop] += transposed_dot(grad, probs.astype(jnp.bfloat16))


def attend_call(kernel, begin, query, key, value, extra, outs, work):
    groups = key.shape[0] // HEAD
    total = key.shape[1]

    def spec(array):
        if array.ndim == 3:
            return pl.BlockSpec((1,) + array.shape[1:], lambda g: (g, 0, 0))
        if array.shape[0] == 1:
            return pl.BlockSpec(array.shape, lambda g: (0, 0))
        return pl.BlockSpec((array.shape[0] // groups, total), lambda g: (g, 0))

    operands = (begin, query, key, value) + extra
    return pl.pallas_call(
        kernel,
        out_shape=outs,
        grid=(groups,),
        in_specs=[spec(array) for array in operands],
        out_specs=[spec(array) for array in outs],
        compiler_params=pltpu.CompilerParams(vmem_limit_bytes=40 << 20),
        cost_estimate=pl.CostEstimate(
            flops=work * query.shape[0] * total * total * 2,
            bytes_accessed=sum(array.size * 2 for array in operands),
            transcendentals=query.shape[0] // HEAD * total * total,
        ),
    )(*operands)


def on_device(
    tokens,
    gain_attn,
    gain_ffn,
    w_query,
    w_key,
    w_value,
    w_output,
    w_router,
    w_gate,
    w_up,
    w_down,
    segments,
    routes,
    cotangent,
):
    bf16, f32 = jnp.bfloat16, jnp.float32
    side = lax.axis_index("tensor")
    core = lax.rem(lax.axis_index("dp"), 2)
    dp = lax.axis_size("dp")
    chips = [[2 * chip + one for chip in range(dp // 2)] for one in (0, 1)]
    total = segments.shape[0]
    mine = tokens.shape[0]
    width = tokens.shape[1]
    half = width // 2
    shard = width // dp
    experts, _, hidden_here = w_gate.shape
    heads_here = w_query.shape[1] // HEAD
    groups_here = w_key.shape[1] // HEAD
    query_cols, key_cols = w_query.shape[1], w_key.shape[1]
    qkv_cols = query_cols + 2 * key_cols
    proj_cols = qkv_cols + w_output.shape[0]

    def swap_core(array):
        return lax.ppermute(array, "dp", [(i, i ^ 1) for i in range(dp)])

    def swap_side(array):
        return lax.ppermute(array, "tensor", [(0, 1), (1, 0)])

    def gather(block):
        own = lax.all_gather(block, "dp", axis=0, tiled=True, axis_index_groups=chips)
        return jnp.concatenate([own, swap_core(own)], axis=0)

    def pair_sum(make):
        theirs = swap_core(make(half).astype(bf16))
        return (make(0) + theirs.astype(f32)).astype(bf16)

    def scatter(block):
        return lax.psum_scatter(
            block, "dp", scatter_dimension=0, tiled=True, axis_index_groups=chips
        ).astype(f32)

    def local_columns(array):
        cut = array.reshape(array.shape[0], dp // 2, 2, shard)
        first, second = cut[:, :, 0, :], cut[:, :, 1, :]
        own = jnp.where(core == 0, first, second)
        other = jnp.where(core == 0, second, first)
        return jnp.concatenate(
            [own.reshape(array.shape[0], half), other.reshape(array.shape[0], half)], axis=1
        )

    def global_columns(array):
        own = array[:, :half].reshape(array.shape[0], dp // 2, shard)
        other = array[:, half:].reshape(array.shape[0], dp // 2, shard)
        first = jnp.where(core == 0, own, other)
        second = jnp.where(core == 0, other, own)
        return jnp.stack([first, second], axis=2).reshape(array.shape[0], width)

    def natural_rows(own, other):
        return jnp.where(
            side == 0,
            jnp.concatenate([own, other], axis=0),
            jnp.concatenate([other, own], axis=0),
        )

    def own_rows(array, axis=0):
        return lax.dynamic_slice_in_dim(array, side * mine, mine, axis)

    def other_rows(array, axis=0):
        return lax.dynamic_slice_in_dim(array, (1 - side) * mine, mine, axis)

    def local_rows(array):
        turned = jnp.concatenate([array[mine:], array[:mine]], axis=0)
        return jnp.where(side == 0, array, turned)

    small = jnp.concatenate([gain_attn[:, None], gain_ffn[:, None], w_router], axis=1)
    small_other = swap_side(small)
    small = jnp.where(
        side == 0,
        jnp.concatenate([small, small_other], axis=0),
        jnp.concatenate([small_other, small], axis=0),
    )
    small_cols = small.shape[1]
    small = jnp.pad(small, ((0, 0), (0, 128 - small_cols)))
    packed = gather(jnp.concatenate([w_query, w_key, w_value, w_output.T, small], axis=1))
    gate_w = gather(w_gate.transpose(1, 0, 2).reshape(shard, experts * hidden_here))
    up_w = gather(w_up.transpose(1, 0, 2).reshape(shard, experts * hidden_here))
    down_w = gather(w_down.transpose(2, 0, 1).reshape(shard, experts * hidden_here))
    qkv_w = packed[:, :qkv_cols]
    out_w = packed[:, qkv_cols:proj_cols]
    gain_one = packed[:, proj_cols].astype(f32)
    gain_two = packed[:, proj_cols + 1].astype(f32)
    router = packed[:, proj_cols + 2 : proj_cols + small_cols]

    tokens = local_columns(tokens)
    cotangent = local_columns(cotangent)
    token_rows = natural_rows(tokens, swap_side(tokens)).astype(f32)
    grad_out = cotangent.astype(f32)
    moe_grad = (RESIDUAL_SCALE * grad_out).astype(bf16)
    moe_grad_rows = jnp.concatenate([moe_grad, swap_side(moe_grad)], axis=0)
    places = positions(segments)
    cosine, sine = rotary(places, HEAD // 2)
    begin = (jnp.arange(total, dtype=jnp.int32) - places)[None, :]
    picks = local_rows(routes)
    inverse_one = lax.rsqrt(jnp.mean(token_rows * token_rows, axis=-1, keepdims=True) + EPSILON)
    base_one = token_rows * inverse_one
    rows_one = (base_one * gain_one).astype(bf16)
    qkv = dot(qkv_w, rows_one, 0, 1)
    queries = rotate(qkv[:query_cols], cosine, sine).astype(bf16)
    keys = rotate(qkv[query_cols : query_cols + key_cols], cosine, sine).astype(bf16)
    values = qkv[query_cols + key_cols :].astype(bf16)
    mixed, log_total = attend_call(
        attend_kernel,
        begin,
        queries,
        keys,
        values,
        (),
        [
            jax.ShapeDtypeStruct((query_cols, total), bf16),
            jax.ShapeDtypeStruct((groups_here, heads_here // groups_here, total), f32),
        ],
        2,
    )
    attn_sent = swap_side(dot(other_rows(mixed, 1), out_w, 0, 1).astype(bf16))
    own_tokens = tokens.astype(f32)
    attn_total = dot(own_rows(mixed, 1), out_w, 0, 1) + attn_sent.astype(f32)
    after_attn = own_tokens + RESIDUAL_SCALE * attn_total
    inverse_two = lax.rsqrt(jnp.mean(after_attn * after_attn, axis=-1, keepdims=True) + EPSILON)
    base_two = after_attn * inverse_two
    normed_two = (base_two * gain_two).astype(bf16)
    rows_two = jnp.concatenate([normed_two, swap_side(normed_two)], axis=0)

    logits = dot(rows_two, router)
    expert_ids = jnp.arange(experts, dtype=jnp.int32)
    routed = jnp.any(picks[:, :, None] == expert_ids[None, None, :], axis=1)
    top_logit = jnp.max(jnp.where(routed, logits, MASKED), axis=-1, keepdims=True)
    powers = jnp.where(routed, jnp.exp(jnp.where(routed, logits - top_logit, 0.0)), 0.0)
    gates = powers / jnp.sum(powers, axis=-1, keepdims=True)
    gates_wide = jnp.broadcast_to(gates[:, :, None], (total, experts, hidden_here))
    gates_wide = gates_wide.reshape(total, experts * hidden_here)
    gate_pre = dot(rows_two, gate_w).astype(bf16)
    up_pre = dot(rows_two, up_w).astype(bf16)
    gate_f, up_f = gate_pre.astype(f32), up_pre.astype(f32)
    sigmoid_gate = jax.nn.sigmoid(gate_f)
    activated = gate_f * sigmoid_gate
    hidden = activated * up_f
    hidden_gated = (gates_wide * hidden).astype(bf16)
    moe_sent = swap_side(dot(hidden_gated[mine:], down_w, 1, 1).astype(bf16))
    moe_total = dot(hidden_gated[:mine], down_w, 1, 1) + moe_sent.astype(f32)
    output = after_attn + RESIDUAL_SCALE * moe_total

    grad_plain = dot(moe_grad_rows, down_w).astype(bf16).astype(f32)
    grad_gates = jnp.sum((hidden * grad_plain).reshape(total, experts, hidden_here), axis=-1)
    grad_hidden = gates_wide * grad_plain
    grad_gate_pre = (
        grad_hidden * up_f * sigmoid_gate * (1.0 + gate_f * (1.0 - sigmoid_gate))
    ).astype(bf16)
    grad_up_pre = (grad_hidden * activated).astype(bf16)
    grad_logits = gates * (grad_gates - jnp.sum(gates * grad_gates, axis=-1, keepdims=True))
    logits_high = grad_logits.astype(bf16)
    logits_low = (grad_logits - logits_high.astype(f32)).astype(bf16)
    logits_pair = jnp.concatenate([logits_high, logits_low], axis=1)
    router_pair = jnp.concatenate([router, router], axis=1)

    def rows_two_back(start):
        rows = slice(start, start + mine)
        part = dot(grad_gate_pre[rows], gate_w, 1, 1) + dot(grad_up_pre[rows], up_w, 1, 1)
        return part + dot(logits_pair[rows], router_pair, 1, 1)

    back_sent = swap_side(rows_two_back(mine).astype(bf16))
    grad_normed_two = rows_two_back(0) + back_sent.astype(f32)
    grad_gate_w = pair_sum(lambda at: dot(rows_two[:, at : at + half], grad_gate_pre, 0, 0))
    grad_up_w = pair_sum(lambda at: dot(rows_two[:, at : at + half], grad_up_pre, 0, 0))
    grad_down_w = pair_sum(lambda at: dot(moe_grad_rows[:, at : at + half], hidden_gated, 0, 0))
    grad_router_pair = dot(rows_two, logits_pair, 0, 0)
    grad_router_w = grad_router_pair[:, :experts] + grad_router_pair[:, experts:]

    grad_gain_two = jnp.sum(grad_normed_two * base_two, axis=0)
    grad_after = grad_out + norm_back(grad_normed_two, base_two, inverse_two, gain_two)
    attn_grad = (RESIDUAL_SCALE * grad_after).astype(bf16)
    attn_grad_rows = natural_rows(attn_grad, swap_side(attn_grad))
    attn_grad_rows, grad_gate_w, grad_up_w, grad_down_w = lax.optimization_barrier(
        (attn_grad_rows, grad_gate_w, grad_up_w, grad_down_w)
    )
    grad_gate, grad_up, grad_down = scatter(grad_gate_w), scatter(grad_up_w), scatter(grad_down_w)
    grad_mixed = dot(out_w, attn_grad_rows, 0, 1).astype(bf16)
    grad_query_rot, grad_key_rot, grad_values = attend_call(
        attend_back_kernel,
        begin,
        queries,
        keys,
        values,
        (log_total, grad_mixed),
        [
            jax.ShapeDtypeStruct((query_cols, total), f32),
            jax.ShapeDtypeStruct((key_cols, total), f32),
            jax.ShapeDtypeStruct((key_cols, total), f32),
        ],
        5,
    )
    grad_qkv = jnp.concatenate(
        [
            rotate(grad_query_rot, cosine, -sine).astype(bf16),
            rotate(grad_key_rot, cosine, -sine).astype(bf16),
            grad_values.astype(bf16),
        ],
        axis=0,
    )
    rows_one_sent = dot(other_rows(grad_qkv, 1), qkv_w, 0, 1)
    rows_one_kept = dot(own_rows(grad_qkv, 1), qkv_w, 0, 1)
    sent_back = swap_side(rows_one_sent.astype(bf16))
    grad_gain_one = jnp.sum(rows_one_sent * other_rows(base_one), axis=0)
    grad_gain_one = grad_gain_one + jnp.sum(rows_one_kept * own_rows(base_one), axis=0)
    small_grads = jnp.concatenate(
        [grad_gain_one[:, None], grad_gain_two[:, None], grad_router_w], axis=1
    )
    small_grads = jnp.pad(small_grads, ((0, 0), (0, 128 - small_cols)))

    def packed_part(at):
        cut = slice(at, at + half)
        return jnp.concatenate(
            [
                dot(rows_one[:, cut], grad_qkv, 0, 1),
                dot(attn_grad_rows[:, cut], mixed, 0, 1),
                small_grads[cut],
            ],
            axis=1,
        )

    packed_grads = scatter(pair_sum(packed_part))
    grad_normed_one = rows_one_kept + sent_back.astype(f32)
    grad_tokens = grad_after + norm_back(
        grad_normed_one, own_rows(base_one), own_rows(inverse_one), gain_one
    )
    grad_query = packed_grads[:, :query_cols]
    grad_key = packed_grads[:, query_cols : query_cols + key_cols]
    grad_value = packed_grads[:, query_cols + key_cols : qkv_cols]
    grad_output = packed_grads[:, qkv_cols:proj_cols].T
    small_grads = packed_grads[:, proj_cols : proj_cols + small_cols]
    piece = shard // 2
    upper, lower = small_grads[:piece], small_grads[piece:]
    small_grads = jnp.where(side == 0, upper, lower) + swap_side(jnp.where(side == 0, lower, upper))

    def expert_block(array):
        return array.reshape(shard, experts, hidden_here)

    return (
        global_columns(output),
        global_columns(grad_tokens),
        small_grads[:, 0],
        small_grads[:, 1],
        grad_query,
        grad_key,
        grad_value,
        grad_output,
        small_grads[:, 2:],
        expert_block(grad_gate).transpose(1, 0, 2),
        expert_block(grad_up).transpose(1, 0, 2),
        expert_block(grad_down).transpose(1, 2, 0),
    )


def solution(mesh):
    in_specs = (
        P(("dp", "tensor"), None),
        P(("dp", "tensor")),
        P(("dp", "tensor")),
        P("dp", "tensor"),
        P("dp", "tensor"),
        P("dp", "tensor"),
        P("tensor", "dp"),
        P(("dp", "tensor"), None),
        P(None, "dp", "tensor"),
        P(None, "dp", "tensor"),
        P(None, "tensor", "dp"),
        P("dp"),
        P("dp", None),
        P(("dp", "tensor"), None),
    )
    out_specs = (
        P(("dp", "tensor"), None),
        P(("dp", "tensor"), None),
        P(("dp", "tensor")),
        P(("dp", "tensor")),
        P("dp", "tensor"),
        P("dp", "tensor"),
        P("dp", "tensor"),
        P("tensor", "dp"),
        P(("dp", "tensor"), None),
        P(None, "dp", "tensor"),
        P(None, "dp", "tensor"),
        P(None, "tensor", "dp"),
    )
    return jax.shard_map(
        on_device, mesh=mesh, in_specs=in_specs, out_specs=out_specs, check_vma=False
    )
```

```python
import jax
import jax.numpy as jnp
from jax import lax
from jax.experimental import pallas as pl
from jax.experimental.pallas import tpu as pltpu
from jax.sharding import PartitionSpec as P

HEAD = 64
BLOCK = 256


EPSILON = 1e-06
RESIDUAL_SCALE = 0.22
SCORE_SCALE = 0.015625
MASKED = -1e30


def positions(doc_ids):
    index_row = jnp.arange(doc_ids.shape[0], dtype=jnp.int32)
    starting = jnp.concatenate([jnp.ones((1,), dtype=jnp.bool_), doc_ids[1:] != doc_ids[:-1]])
    seg_begin = lax.cummax(jnp.where(starting, index_row, jnp.zeros_like(index_row)), axis=0)
    return index_row - seg_begin


def rotary(places, half_width):
    freqs = 10000.0 ** (-jnp.arange(half_width, dtype=jnp.float32) / half_width)
    angles = freqs[:, None] * places.astype(jnp.float32)[None, :]
    return (jnp.cos(angles), jnp.sin(angles))


def rotate(values, cosine, sine):
    heads = values.reshape(values.shape[0] // HEAD, 2, HEAD // 2, values.shape[1])
    first_half, second_half = heads[:, 0], heads[:, 1]
    return jnp.stack(
        [first_half * cosine - second_half * sine, second_half * cosine + first_half * sine],
        axis=1,
    ).reshape(values.shape)


def norm_back(grad_normed, base, inverse, gain):
    scaled = grad_normed * gain
    return inverse * scaled - base * inverse * jnp.mean(scaled * base, axis=-1, keepdims=True)


def dot(left, right, left_dim=1, right_dim=0):
    return lax.dot_general(
        left, right, (((left_dim,), (right_dim,)), ((), ())), preferred_element_type=jnp.float32
    )


def transposed_dot(left, right):
    return dot(left, right, 1, 1)


def allowed_keys(begin_ref, start, stop):
    shape = (stop, stop - start)
    key = lax.broadcasted_iota(jnp.int32, shape, 0)
    query = lax.broadcasted_iota(jnp.int32, shape, 1) + start
    return (key >= begin_ref[:, start:stop]) & (key <= query)


def attend_kernel(begin_ref, query_ref, key_ref, value_ref, mixed_ref, lse_ref):
    total = key_ref.shape[1]
    keys = (key_ref[...].astype(jnp.float32) * SCORE_SCALE).T.astype(jnp.bfloat16)
    for start in range(0, total, BLOCK):
        stop = start + BLOCK
        allowed = allowed_keys(begin_ref, start, stop)
        for head in range(query_ref.shape[0] // HEAD):
            rows = slice(head * HEAD, (head + 1) * HEAD)
            scores = dot(keys[:stop], query_ref[rows, start:stop])
            scores = jnp.where(allowed, scores, MASKED)
            top = jnp.max(scores, axis=0, keepdims=True)
            expo = jnp.exp(scores - top)
            denom = jnp.sum(expo, axis=0, keepdims=True)
            probs = (expo * (1.0 / denom)).astype(jnp.bfloat16)
            mixed_ref[rows, start:stop] = dot(value_ref[:, :stop], probs).astype(jnp.bfloat16)
            lse_ref[0, head : head + 1, start:stop] = top + jnp.log(denom)


def attend_back_kernel(
    begin_ref,
    query_ref,
    key_ref,
    value_ref,
    lse_ref,
    grad_ref,
    grad_query_ref,
    grad_key_ref,
    grad_value_ref,
):
    total = key_ref.shape[1]
    keys = (key_ref[...].astype(jnp.float32) * SCORE_SCALE).T.astype(jnp.bfloat16)
    values = value_ref[...].astype(jnp.float32).T.astype(jnp.bfloat16)
    grad_key_ref[...] = jnp.zeros_like(grad_key_ref)
    grad_value_ref[...] = jnp.zeros_like(grad_value_ref)
    for start in range(0, total, BLOCK):
        stop = start + BLOCK
        allowed = allowed_keys(begin_ref, start, stop)
        for head in range(query_ref.shape[0] // HEAD):
            rows = slice(head * HEAD, (head + 1) * HEAD)
            query = query_ref[rows, start:stop]
            grad = grad_ref[rows, start:stop]
            scores = dot(keys[:stop], query) - lse_ref[0, head : head + 1, start:stop]
            probs = jnp.exp(jnp.where(allowed, scores, MASKED))
            grad_probs = dot(values[:stop], grad)
            delta = jnp.sum(probs * grad_probs, axis=0, keepdims=True)
            grad_scores = (probs * (grad_probs - delta)).astype(jnp.bfloat16)
            grad_query_ref[rows, start:stop] = SCORE_SCALE * dot(key_ref[:, :stop], grad_scores)
            grad_key_ref[:, :stop] += SCORE_SCALE * transposed_dot(query, grad_scores)
            grad_value_ref[:, :stop] += transposed_dot(grad, probs.astype(jnp.bfloat16))


def attend_call(kernel, begin, query, key, value, extra, outs, work):
    groups = key.shape[0] // HEAD
    total = key.shape[1]

    def spec(array):
        if array.ndim == 3:
            return pl.BlockSpec((1,) + array.shape[1:], lambda g: (g, 0, 0))
        if array.shape[0] == 1:
            return pl.BlockSpec(array.shape, lambda g: (0, 0))
        return pl.BlockSpec((array.shape[0] // groups, total), lambda g: (g, 0))

    operands = (begin, query, key, value) + extra
    return pl.pallas_call(
        kernel,
        out_shape=outs,
        grid=(groups,),
        in_specs=[spec(array) for array in operands],
        out_specs=[spec(array) for array in outs],
        compiler_params=pltpu.CompilerParams(vmem_limit_bytes=40 << 20),
        cost_estimate=pl.CostEstimate(
            flops=work * query.shape[0] * total * total * 2,
            bytes_accessed=sum(array.size * 2 for array in operands),
            transcendentals=query.shape[0] // HEAD * total * total,
        ),
    )(*operands)


def pick_column(gates_ref):
    expert = lax.broadcasted_iota(jnp.int32, gates_ref.shape, 1) == pl.program_id(0)
    return expert, jnp.sum(jnp.where(expert, gates_ref[...], 0.0), axis=1, keepdims=True)


def expert_kernel(rows_ref, gate_w_ref, up_w_ref, gates_ref, gate_ref, up_ref, hidden_ref):
    _, gate_column = pick_column(gates_ref)
    for start in range(0, rows_ref.shape[0], BLOCK):
        cut = slice(start, start + BLOCK)
        gate = dot(rows_ref[cut, :], gate_w_ref[...])
        up = dot(rows_ref[cut, :], up_w_ref[...])
        gate_ref[cut, :] = gate.astype(jnp.bfloat16)
        up_ref[cut, :] = up.astype(jnp.bfloat16)
        hidden = gate * jax.nn.sigmoid(gate) * up
        hidden_ref[cut, :] = (gate_column[cut] * hidden).astype(jnp.bfloat16)


def expert_back_kernel(
    grad_rows_ref,
    down_w_ref,
    gate_ref,
    up_ref,
    gates_ref,
    grad_gate_ref,
    grad_up_ref,
    grad_gates_ref,
):
    expert, gate_column = pick_column(gates_ref)

    @pl.when(pl.program_id(0) == 0)
    def _():
        grad_gates_ref[...] = jnp.zeros_like(grad_gates_ref)

    for start in range(0, grad_rows_ref.shape[0], BLOCK):
        cut = slice(start, start + BLOCK)
        plain = dot(grad_rows_ref[cut, :], down_w_ref[...])
        gate = gate_ref[cut, :].astype(jnp.float32)
        up = up_ref[cut, :].astype(jnp.float32)
        sigmoid_gate = jax.nn.sigmoid(gate)
        activated = gate * sigmoid_gate
        grad_column = jnp.sum(activated * up * plain, axis=1, keepdims=True)
        grad_gates_ref[cut, :] += jnp.where(expert[cut], grad_column, 0.0)
        grad_hidden = gate_column[cut] * plain
        slope = sigmoid_gate * (1.0 + gate * (1.0 - sigmoid_gate))
        grad_gate_ref[cut, :] = (grad_hidden * up * slope).astype(jnp.bfloat16)
        grad_up_ref[cut, :] = (grad_hidden * activated).astype(jnp.bfloat16)


def expert_call(kernel, operands, outs, experts, work):
    def spec(array):
        if array.shape[1] < experts * BLOCK:
            return pl.BlockSpec(array.shape, lambda e: (0, 0))
        return pl.BlockSpec((array.shape[0], array.shape[1] // experts), lambda e: (0, e))

    return pl.pallas_call(
        kernel,
        out_shape=outs,
        grid=(experts,),
        in_specs=[spec(array) for array in operands],
        out_specs=[spec(array) for array in outs],
        compiler_params=pltpu.CompilerParams(vmem_limit_bytes=40 << 20),
        cost_estimate=pl.CostEstimate(
            flops=2 * work,
            bytes_accessed=sum(array.size * 2 for array in operands),
            transcendentals=outs[0].size,
        ),
    )(*operands)


def on_device(
    tokens,
    gain_attn,
    gain_ffn,
    w_query,
    w_key,
    w_value,
    w_output,
    w_router,
    w_gate,
    w_up,
    w_down,
    segments,
    routes,
    cotangent,
):
    bf16, f32 = jnp.bfloat16, jnp.float32
    side = lax.axis_index("tensor")
    core = lax.rem(lax.axis_index("dp"), 2)
    near = lax.rem(lax.axis_index("dp") // 2, 2)
    dp = lax.axis_size("dp")
    far = dp // 4
    lines = [[4 * step + first for step in range(far)] for first in range(4)]
    total = segments.shape[0]
    mine = tokens.shape[0]
    width = tokens.shape[1]
    half = width // 2
    quarter = width // 4
    shard = width // dp
    experts, _, hidden_here = w_gate.shape
    heads_here = w_query.shape[1] // HEAD
    groups_here = w_key.shape[1] // HEAD
    query_cols, key_cols = w_query.shape[1], w_key.shape[1]
    qkv_cols = query_cols + 2 * key_cols
    proj_cols = qkv_cols + w_output.shape[0]

    def swap_core(array):
        return lax.ppermute(array, "dp", [(i, i ^ 1) for i in range(dp)])

    def swap_side(array):
        return lax.ppermute(array, "tensor", [(0, 1), (1, 0)])

    def swap_near(array):
        return lax.ppermute(array, "dp", [(i, i ^ 2) for i in range(dp)])

    def gather(block):
        own = lax.all_gather(block, "dp", axis=0, tiled=True, axis_index_groups=lines)
        own = jnp.concatenate([own, swap_near(own)], axis=0)
        return jnp.concatenate([own, swap_core(own)], axis=0)

    def pair_sum(make):
        theirs = swap_core(make(half).astype(bf16))
        return (make(0) + theirs.astype(f32)).astype(bf16)

    def near_sum(block):
        theirs = swap_near(block[quarter:])
        return (block[:quarter].astype(f32) + theirs.astype(f32)).astype(bf16)

    def scatter(block):
        return lax.psum_scatter(
            block, "dp", scatter_dimension=0, tiled=True, axis_index_groups=lines
        ).astype(f32)

    def own_first(flag, array, axis):
        first = lax.index_in_dim(array, 0, axis, keepdims=False)
        second = lax.index_in_dim(array, 1, axis, keepdims=False)
        return jnp.where(flag == 0, first, second), jnp.where(flag == 0, second, first)

    def local_columns(array):
        cut = array.reshape(array.shape[0], far, 2, 2, shard)
        pieces = []
        for side_piece in own_first(core, cut, 3):
            pieces.extend(own_first(near, side_piece, 2))
        return jnp.concatenate([one.reshape(array.shape[0], quarter) for one in pieces], axis=1)

    def global_columns(array):
        cut = array.reshape(array.shape[0], 2, 2, far, shard)
        halves = own_first(core, cut, 1)
        halves = [jnp.stack(own_first(near, one, 1), axis=2) for one in halves]
        return jnp.stack(halves, axis=3).reshape(array.shape[0], width)

    def natural_rows(own, other):
        return jnp.where(
            side == 0,
            jnp.concatenate([own, other], axis=0),
            jnp.concatenate([other, own], axis=0),
        )

    def own_rows(array, axis=0):
        return lax.dynamic_slice_in_dim(array, side * mine, mine, axis)

    def other_rows(array, axis=0):
        return lax.dynamic_slice_in_dim(array, (1 - side) * mine, mine, axis)

    def local_rows(array):
        turned = jnp.concatenate([array[mine:], array[:mine]], axis=0)
        return jnp.where(side == 0, array, turned)

    small = jnp.concatenate([gain_attn[:, None], gain_ffn[:, None], w_router], axis=1)
    small_other = swap_side(small)
    small = jnp.where(
        side == 0,
        jnp.concatenate([small, small_other], axis=0),
        jnp.concatenate([small_other, small], axis=0),
    )
    small_cols = small.shape[1]
    small = jnp.pad(small, ((0, 0), (0, 128 - small_cols)))
    packed = gather(jnp.concatenate([w_query, w_key, w_value, w_output.T, small], axis=1))
    gate_w = gather(w_gate.transpose(1, 0, 2).reshape(shard, experts * hidden_here))
    up_w = gather(w_up.transpose(1, 0, 2).reshape(shard, experts * hidden_here))
    down_w = gather(w_down.transpose(2, 0, 1).reshape(shard, experts * hidden_here))
    qkv_w = packed[:, :qkv_cols]
    out_w = packed[:, qkv_cols:proj_cols]
    gain_one = packed[:, proj_cols].astype(f32)
    gain_two = packed[:, proj_cols + 1].astype(f32)
    router = packed[:, proj_cols + 2 : proj_cols + small_cols]

    tokens = local_columns(tokens)
    cotangent = local_columns(cotangent)
    token_rows = natural_rows(tokens, swap_side(tokens)).astype(f32)
    grad_out = cotangent.astype(f32)
    moe_grad = (RESIDUAL_SCALE * grad_out).astype(bf16)
    moe_grad_rows = jnp.concatenate([moe_grad, swap_side(moe_grad)], axis=0)
    places = positions(segments)
    cosine, sine = rotary(places, HEAD // 2)
    begin = (jnp.arange(total, dtype=jnp.int32) - places)[None, :]
    picks = local_rows(routes)
    inverse_one = lax.rsqrt(jnp.mean(token_rows * token_rows, axis=-1, keepdims=True) + EPSILON)
    base_one = token_rows * inverse_one
    rows_one = (base_one * gain_one).astype(bf16)
    qkv = dot(qkv_w, rows_one, 0, 1)
    queries = rotate(qkv[:query_cols], cosine, sine).astype(bf16)
    keys = rotate(qkv[query_cols : query_cols + key_cols], cosine, sine).astype(bf16)
    values = qkv[query_cols + key_cols :].astype(bf16)
    mixed, log_total = attend_call(
        attend_kernel,
        begin,
        queries,
        keys,
        values,
        (),
        [
            jax.ShapeDtypeStruct((query_cols, total), bf16),
            jax.ShapeDtypeStruct((groups_here, heads_here // groups_here, total), f32),
        ],
        2,
    )
    attn_sent = swap_side(dot(other_rows(mixed, 1), out_w, 0, 1).astype(bf16))
    own_tokens = tokens.astype(f32)
    attn_total = dot(own_rows(mixed, 1), out_w, 0, 1) + attn_sent.astype(f32)
    after_attn = own_tokens + RESIDUAL_SCALE * attn_total
    inverse_two = lax.rsqrt(jnp.mean(after_attn * after_attn, axis=-1, keepdims=True) + EPSILON)
    base_two = after_attn * inverse_two
    normed_two = (base_two * gain_two).astype(bf16)
    rows_two = jnp.concatenate([normed_two, swap_side(normed_two)], axis=0)

    logits = dot(rows_two, router)
    expert_ids = jnp.arange(experts, dtype=jnp.int32)
    routed = jnp.any(picks[:, :, None] == expert_ids[None, None, :], axis=1)
    top_logit = jnp.max(jnp.where(routed, logits, MASKED), axis=-1, keepdims=True)
    powers = jnp.where(routed, jnp.exp(jnp.where(routed, logits - top_logit, 0.0)), 0.0)
    gates = powers / jnp.sum(powers, axis=-1, keepdims=True)
    wide = jax.ShapeDtypeStruct((total, experts * hidden_here), bf16)
    matmul = total * width * experts * hidden_here
    gate_pre, up_pre, hidden_gated = expert_call(
        expert_kernel, (rows_two, gate_w, up_w, gates), [wide] * 3, experts, 2 * matmul
    )
    moe_sent = swap_side(dot(hidden_gated[mine:], down_w, 1, 1).astype(bf16))
    moe_total = dot(hidden_gated[:mine], down_w, 1, 1) + moe_sent.astype(f32)
    output = after_attn + RESIDUAL_SCALE * moe_total

    grad_gate_pre, grad_up_pre, grad_gates = expert_call(
        expert_back_kernel,
        (moe_grad_rows, down_w, gate_pre, up_pre, gates),
        [wide, wide, jax.ShapeDtypeStruct((total, experts), f32)],
        experts,
        matmul,
    )
    grad_logits = gates * (grad_gates - jnp.sum(gates * grad_gates, axis=-1, keepdims=True))
    logits_high = grad_logits.astype(bf16)
    logits_low = (grad_logits - logits_high.astype(f32)).astype(bf16)
    logits_pair = jnp.concatenate([logits_high, logits_low], axis=1)
    router_pair = jnp.concatenate([router, router], axis=1)

    def rows_two_back(start):
        rows = slice(start, start + mine)
        part = dot(grad_gate_pre[rows], gate_w, 1, 1) + dot(grad_up_pre[rows], up_w, 1, 1)
        return part + dot(logits_pair[rows], router_pair, 1, 1)

    back_sent = swap_side(rows_two_back(mine).astype(bf16))
    grad_normed_two = rows_two_back(0) + back_sent.astype(f32)
    grad_gate_w = pair_sum(lambda at: dot(rows_two[:, at : at + half], grad_gate_pre, 0, 0))
    grad_up_w = pair_sum(lambda at: dot(rows_two[:, at : at + half], grad_up_pre, 0, 0))
    grad_down_w = pair_sum(lambda at: dot(moe_grad_rows[:, at : at + half], hidden_gated, 0, 0))
    grad_router_pair = dot(rows_two, logits_pair, 0, 0)
    grad_router_w = grad_router_pair[:, :experts] + grad_router_pair[:, experts:]

    grad_gain_two = jnp.sum(grad_normed_two * base_two, axis=0)
    grad_after = grad_out + norm_back(grad_normed_two, base_two, inverse_two, gain_two)
    attn_grad = (RESIDUAL_SCALE * grad_after).astype(bf16)
    attn_grad_rows = natural_rows(attn_grad, swap_side(attn_grad))
    attn_grad_rows, grad_gate_w, grad_up_w, grad_down_w = lax.optimization_barrier(
        (attn_grad_rows, grad_gate_w, grad_up_w, grad_down_w)
    )
    grad_gate = scatter(near_sum(grad_gate_w))
    grad_up = scatter(near_sum(grad_up_w))
    grad_down = scatter(near_sum(grad_down_w))
    grad_mixed = dot(out_w, attn_grad_rows, 0, 1).astype(bf16)
    grad_query_rot, grad_key_rot, grad_values = attend_call(
        attend_back_kernel,
        begin,
        queries,
        keys,
        values,
        (log_total, grad_mixed),
        [
            jax.ShapeDtypeStruct((query_cols, total), f32),
            jax.ShapeDtypeStruct((key_cols, total), f32),
            jax.ShapeDtypeStruct((key_cols, total), f32),
        ],
        5,
    )
    grad_qkv = jnp.concatenate(
        [
            rotate(grad_query_rot, cosine, -sine).astype(bf16),
            rotate(grad_key_rot, cosine, -sine).astype(bf16),
            grad_values.astype(bf16),
        ],
        axis=0,
    )
    rows_one_sent = dot(other_rows(grad_qkv, 1), qkv_w, 0, 1)
    rows_one_kept = dot(own_rows(grad_qkv, 1), qkv_w, 0, 1)
    sent_back = swap_side(rows_one_sent.astype(bf16))
    grad_gain_one = jnp.sum(rows_one_sent * other_rows(base_one), axis=0)
    grad_gain_one = grad_gain_one + jnp.sum(rows_one_kept * own_rows(base_one), axis=0)
    small_grads = jnp.concatenate(
        [grad_gain_one[:, None], grad_gain_two[:, None], grad_router_w], axis=1
    )
    small_grads = jnp.pad(small_grads, ((0, 0), (0, 128 - small_cols)))

    def packed_part(at):
        cut = slice(at, at + half)
        return jnp.concatenate(
            [
                dot(rows_one[:, cut], grad_qkv, 0, 1),
                dot(attn_grad_rows[:, cut], mixed, 0, 1),
                small_grads[cut],
            ],
            axis=1,
        )

    packed_grads = near_sum(pair_sum(packed_part))
    packed_grads, grad_gate, grad_up, grad_down = lax.optimization_barrier(
        (packed_grads, grad_gate, grad_up, grad_down)
    )
    packed_grads = scatter(packed_grads)
    grad_normed_one = rows_one_kept + sent_back.astype(f32)
    grad_tokens = grad_after + norm_back(
        grad_normed_one, own_rows(base_one), own_rows(inverse_one), gain_one
    )
    grad_query = packed_grads[:, :query_cols]
    grad_key = packed_grads[:, query_cols : query_cols + key_cols]
    grad_value = packed_grads[:, query_cols + key_cols : qkv_cols]
    grad_output = packed_grads[:, qkv_cols:proj_cols].T
    small_grads = packed_grads[:, proj_cols : proj_cols + small_cols]
    piece = shard // 2
    upper, lower = small_grads[:piece], small_grads[piece:]
    small_grads = jnp.where(side == 0, upper, lower) + swap_side(jnp.where(side == 0, lower, upper))

    def expert_block(array):
        return array.reshape(shard, experts, hidden_here)

    return (
        global_columns(output),
        global_columns(grad_tokens),
        small_grads[:, 0],
        small_grads[:, 1],
        grad_query,
        grad_key,
        grad_value,
        grad_output,
        small_grads[:, 2:],
        expert_block(grad_gate).transpose(1, 0, 2),
        expert_block(grad_up).transpose(1, 0, 2),
        expert_block(grad_down).transpose(1, 2, 0),
    )


def solution(mesh):
    in_specs = (
        P(("dp", "tensor"), None),
        P(("dp", "tensor")),
        P(("dp", "tensor")),
        P("dp", "tensor"),
        P("dp", "tensor"),
        P("dp", "tensor"),
        P("tensor", "dp"),
        P(("dp", "tensor"), None),
        P(None, "dp", "tensor"),
        P(None, "dp", "tensor"),
        P(None, "tensor", "dp"),
        P("dp"),
        P("dp", None),
        P(("dp", "tensor"), None),
    )
    out_specs = (
        P(("dp", "tensor"), None),
        P(("dp", "tensor"), None),
        P(("dp", "tensor")),
        P(("dp", "tensor")),
        P("dp", "tensor"),
        P("dp", "tensor"),
        P("dp", "tensor"),
        P("tensor", "dp"),
        P(("dp", "tensor"), None),
        P(None, "dp", "tensor"),
        P(None, "dp", "tensor"),
        P(None, "tensor", "dp"),
    )
    return jax.shard_map(
        on_device, mesh=mesh, in_specs=in_specs, out_specs=out_specs, check_vma=False
    )
```
